32 devices in a mesh: dp: 2 (over x), blk: 16 (over z, y, core).
Axes of the slice: x: 2, y: 2, z: 4, core: 2. Of those that a mesh axis runs over, the one named last changes fastest.
Arguments:
- tokens: bfloat16 [24576, 16384], P('dp', 'blk'), may hold values from -6 to 6
- left: bfloat16 [128, 128, 128], P('blk'), may hold values from -0.5 to 0.5
- right: bfloat16 [128, 128, 128], P('blk'), may hold values from -0.5 to 0.5
- cotangent: bfloat16 [24576, 16384], P('dp', 'blk'), may hold values from -6 to 6
- keep_mask: int32 [128, 24576], P('blk', 'dp'), may hold values 0 or 1
- channel_order: int32 [128], replicated, may hold values from 0 to 127, each once
Outputs:
- mixed: bfloat16 [24576, 16384], P('dp', 'blk')
- grad_tokens: bfloat16 [24576, 16384], P('dp', 'blk')
- grad_left: float32 [128, 128, 128], P('blk')
- grad_right: float32 [128, 128, 128], P('blk')
The draws below stay inside these ranges and needn't reach their ends.
Inputs may be any that keep to these rules, and one draw needn't show every extreme that they name: `channel_order`: each of 0 to 127 appears once.
All inputs are finite; a program needn't handle non-finite values. No bound on the sum of `keep_mask` on one device may be relied on, other than what follows from the above.
Results may differ from the reference program's by a relative error of at most 0.0075.
Values may be sent and summed in bfloat16 or wider, within the bound.
No kernel may reach another device: no remote copies, remote signals or barrier semaphores. Data moves between devices by JAX's collectives and lax.ppermute only.
A program may use at most 384 MiB of HBM per device.

```python
import math
import jax
import jax.numpy as jnp
from jax import lax

NB = 128
BS = 128
TOKENS = 24576
WIDTH = 16384


def touch_ends(drawn, rng, least, top_value):
    dims = drawn.shape
    spot = [jax.random.randint(jax.random.fold_in(rng, axis), (), 0, dims[axis]) for axis in range(len(dims))]
    drawn = drawn.at[tuple(spot)].set(least)
    longest = dims.index(max(dims))
    spot[longest] = (spot[longest] + 1) % dims[longest]
    return drawn.at[tuple(spot)].set(top_value)


def steps_of(rng, shape, shards, low, largest):
    def one(dim, parts):
        steps = jax.random.uniform(jax.random.fold_in(jax.random.fold_in(rng, 6), dim), (parts,), jnp.float32, low / len(shards), largest / len(shards))
        return jnp.repeat(jnp.exp(steps), shape[dim] // parts).reshape((-1,) + (1,) * (len(shape) - dim - 1))

    gain = one(*shards[0])
    for cut in shards[1:]:
        gain = gain * one(*cut)
    return gain


def normal_values(rng, dims, scale, reach, cuts=(), kind=jnp.bfloat16):
    gain = steps_of(rng, dims, cuts, -0.22, 0.18) if cuts else 1.0
    drawn = jax.random.normal(rng, dims, jnp.float32) * scale * gain
    return jnp.minimum(jnp.maximum(drawn, -reach), reach).astype(kind)


def setup_inputs(seed: int = 0) -> dict:
    splits = jax.random.split(jax.random.key(seed), 7)
    tokens = normal_values(splits[0], (TOKENS, WIDTH), 1.0, 6.0, ((0, 2), (1, 16)))
    left = normal_values(splits[1], (NB, BS, BS), BS ** -0.5, 0.5, ((0, 16),))
    right = normal_values(splits[2], (BS, NB, NB), NB ** -0.5, 0.5, ((0, 16),))
    cotangent = normal_values(splits[3], (TOKENS, WIDTH), 1.0, 6.0, ((0, 2), (1, 16)))
    keep_mask = touch_ends((jax.random.randint(splits[4], (BS, TOKENS), 0, 10) < 9).astype(jnp.int32), jax.random.fold_in(splits[4], 1), 0, 1)
    channel_order = jax.random.permutation(splits[5], BS).astype(jnp.int32)
    return dict(tokens=tokens, left=left, right=right, cotangent=cotangent, keep_mask=keep_mask, channel_order=channel_order)


keep_rate = 0.9

def normal_parts(value):
    normal_cdf = 0.5 * (1.0 + jax.scipy.special.erf(value / math.sqrt(2.0)))
    normal_pdf = jnp.exp(-0.5 * value * value) / math.sqrt(2.0 * math.pi)
    return (normal_cdf, normal_pdf)

def reference(tokens, left, right, cotangent, keep_mask, channel_order):
    width_all = NB * BS
    block_rows = math.gcd(TOKENS, 1024)
    block_count = TOKENS // block_rows
    inverse = jnp.argsort(channel_order).astype(jnp.int32)
    left_wide = left.astype(jnp.float32)
    right_wide = right.astype(jnp.float32)

    def step_forward(carry, block_index):
        grad_l, grad_r = carry
        row_start = (block_index * block_rows).astype(jnp.int32)
        source = lax.dynamic_slice_in_dim(tokens, row_start, block_rows, 0)
        upstream = lax.dynamic_slice_in_dim(cotangent, row_start, block_rows, 0)
        kept = lax.dynamic_slice_in_dim(keep_mask, row_start, block_rows, 1).T.astype(jnp.float32) / keep_rate
        block_shaped = source.reshape(block_rows, NB, BS)
        permuted = block_shaped[:, :, channel_order].astype(jnp.float32)
        first_out = jnp.einsum('tbk,bko->tbo', permuted, left_wide).astype(jnp.bfloat16)
        first_factor_expanded = first_out.astype(jnp.float32)
        mixing = jnp.einsum('tbj,jbi->tji', first_factor_expanded, right_wide)
        normal_cdf, normal_pdf = normal_parts(mixing)
        branch = kept[:, :, None] * mixing * normal_cdf
        mixed_rows = (source.astype(jnp.float32) + branch.reshape(block_rows, width_all)).astype(jnp.bfloat16)
        up_projection_gradient = upstream.reshape(block_rows, BS, NB).astype(jnp.float32)
        grad_mix = (up_projection_gradient * kept[:, :, None] * (normal_cdf + mixing * normal_pdf)).astype(jnp.bfloat16)
        grad_mix_wide = grad_mix.astype(jnp.float32)
        grad_r = grad_r + jnp.einsum('tbj,tji->jbi', first_factor_expanded, grad_mix_wide)
        first_factor_gradient = jnp.einsum('tji,jbi->tbj', grad_mix_wide, right_wide).astype(jnp.bfloat16)
        grad_first_wide = first_factor_gradient.astype(jnp.float32)
        grad_l = grad_l + jnp.einsum('tbk,tbo->bko', permuted, grad_first_wide)
        grad_perm = jnp.einsum('tbo,bko->tbk', grad_first_wide, left_wide)
        grad_in = grad_perm[:, :, inverse].reshape(block_rows, width_all)
        gradient_row_slices = (upstream.astype(jnp.float32) + grad_in).astype(jnp.bfloat16)
        return ((grad_l, grad_r), (mixed_rows, gradient_row_slices))
    start_carry = (jnp.zeros((NB, BS, BS), jnp.float32), jnp.zeros((BS, NB, NB), jnp.float32))
    (grad_l, grad_r), (mixed_all, grad_all) = lax.scan(step_forward, start_carry, jnp.arange(block_count, dtype=jnp.int32))
    factor = 1.0 / math.sqrt(TOKENS)
    mixed = mixed_all.reshape(TOKENS, width_all)
    grad_tokens = grad_all.reshape(TOKENS, width_all)
    return (mixed, grad_tokens, grad_l * factor, grad_r * factor)
```

```python
import functools
import math

import jax
import jax.numpy as jnp
from jax import lax
from jax.experimental import pallas as pl
from jax.experimental.pallas import tpu as pltpu
from jax.sharding import PartitionSpec as P

keep_rate = 0.9
CHUNKS = 8
TILE = 512
VMEM_LIMIT = 44 * 1024 * 1024
NT = (((1,), (1,)), ((), ()))
TN = (((0,), (0,)), ((), ()))
NN = (((1,), (0,)), ((), ()))


def dot(lhs, rhs, dims):
    return lax.dot_general(lhs, rhs, dims, preferred_element_type=jnp.float32)


class Plan:
    def __init__(self, rows, own, order, devices):
        self.rows, self.own, self.order, self.devices = rows, own, order, devices
        self.direct = (2 * own) % 16 == 0 and own >= 2
        self.pair = 2 if self.direct else own
        self.pairs = own // self.pair
        self.slots = devices if self.direct else 1
        self.height = devices * own * own
        self.slot_height = self.height // self.slots
        self.width = own * order
        self.chunks = CHUNKS
        self.chunk = rows // self.chunks
        self.tile = math.gcd(self.chunk, TILE)
        self.steps = self.chunk // self.tile

    def token_spec(self, chunk):
        return pl.BlockSpec((self.tile, self.width), lambda i: (chunk * self.steps + i, 0))

    def slot_specs(self):
        return [pl.BlockSpec((self.slot_height, self.tile), lambda i: (0, i))] * self.slots

    def slot_shapes(self):
        return [jax.ShapeDtypeStruct((self.slot_height, self.chunk), jnp.bfloat16)] * self.slots

    def pair_rows(self, refs, pair):
        if self.pairs == 1 and self.slots == 1:
            return refs[0][...]
        size = self.pair * self.own
        return jnp.concatenate([ref[pair * size : (pair + 1) * size, :] for ref in refs], axis=0)


def whole(array):
    zeros = (0,) * array.ndim
    return pl.BlockSpec(array.shape, lambda i: zeros)


def call(body, plan, ins, in_specs, outs, out_specs, aliases, flops, scratch=()):
    size = sum(math.prod(o.shape) * o.dtype.itemsize for o in outs[: plan.slots]) * 4
    return pl.pallas_call(
        body,
        out_shape=outs,
        grid=(plan.steps,),
        in_specs=in_specs,
        out_specs=out_specs,
        scratch_shapes=scratch,
        input_output_aliases=aliases,
        compiler_params=pltpu.CompilerParams(vmem_limit_bytes=VMEM_LIMIT),
        cost_estimate=pl.CostEstimate(flops=flops, bytes_accessed=size, transcendentals=0),
    )(*ins)


def first_factor(plan, chunk, tokens, wide_left):
    def body(tokens_ref, left_ref, *out_refs):
        product = dot(left_ref[...], tokens_ref[...], NT).astype(jnp.bfloat16)
        for slot, ref in enumerate(out_refs):
            ref[...] = product[slot * plan.slot_height : (slot + 1) * plan.slot_height, :]

    return call(
        body,
        plan,
        (tokens, wide_left),
        [plan.token_spec(chunk), whole(wide_left)],
        plan.slot_shapes(),
        plan.slot_specs(),
        {},
        2 * plan.height * plan.width * plan.chunk,
    )


def second_factor(plan, chunk, received, tokens, cotangent, keep_mask, spread, wide_right, state):
    slots, span = plan.slots, plan.pair * plan.order

    def body(*refs):
        got = refs[:slots]
        tokens_ref, cotangent_ref, mask_ref, spread_ref, right_ref = refs[slots : slots + 5]
        outs = refs[len(refs) - slots - 2 :]
        sent, mixed_ref, total_ref = outs[:slots], outs[slots], outs[slots + 1]

        @pl.when(pl.program_id(0) == 0)
        def _():
            if chunk == 0:
                total_ref[...] = jnp.zeros_like(total_ref)
            else:
                total_ref[...] = refs[slots + 6][...]

        mask = mask_ref[...].astype(jnp.float32).astype(jnp.bfloat16)
        for pair in range(plan.pairs):
            columns = slice(pair * span, (pair + 1) * span)
            kept = dot(mask, spread_ref[:, columns], TN) * jnp.float32(1.0 / keep_rate)
            rows = plan.pair_rows(got, pair)
            mixing = dot(rows, right_ref[pair], TN)
            cdf = 0.5 * (1.0 + lax.erf(mixing * jnp.float32(1.0 / math.sqrt(2.0))))
            pdf = jnp.exp(-0.5 * mixing * mixing) * jnp.float32(1.0 / math.sqrt(2.0 * math.pi))
            branch = kept * mixing * cdf
            mixed_ref[:, columns] = (tokens_ref[:, columns].astype(jnp.float32) + branch).astype(jnp.bfloat16)
            grad_mix = (cotangent_ref[:, columns].astype(jnp.float32) * kept * (cdf + mixing * pdf)).astype(
                jnp.bfloat16
            )
            total_ref[pair] += dot(rows, grad_mix, NN)
            back = dot(right_ref[pair], grad_mix, NT).astype(jnp.bfloat16)
            if plan.pairs == 1 and slots == 1:
                sent[0][...] = back
            else:
                size = plan.pair * plan.own
                for slot, ref in enumerate(sent):
                    ref[pair * size : (pair + 1) * size, :] = back[slot * size : (slot + 1) * size, :]

    ins = (*received, tokens, cotangent, keep_mask, spread, wide_right)
    in_specs = [
        *plan.slot_specs(),
        plan.token_spec(chunk),
        plan.token_spec(chunk),
        pl.BlockSpec((plan.own, plan.tile), lambda i: (0, chunk * plan.steps + i)),
        whole(spread),
        whole(wide_right),
    ]
    aliases = {}
    if state is not None:
        aliases = {len(ins): slots, len(ins) + 1: slots + 1}
        ins = (*ins, *state)
        in_specs += [pl.BlockSpec(memory_space=pl.ANY), whole(state[1])]
    outs = [
        *plan.slot_shapes(),
        jax.ShapeDtypeStruct(tokens.shape, jnp.bfloat16),
        jax.ShapeDtypeStruct((plan.pairs, plan.pair * plan.order, span), jnp.float32),
    ]
    out_specs = [*plan.slot_specs(), plan.token_spec(chunk), whole(outs[-1])]
    flops = 6 * plan.height * span * plan.chunk * 4
    result = call(body, plan, ins, in_specs, outs, out_specs, aliases, flops)
    return result[:slots], (result[slots], result[slots + 1])


def first_factor_back(plan, chunk, received, tokens, cotangent, wide_left, state):
    slots, own, order = plan.slots, plan.own, plan.order

    def body(*refs):
        got = refs[:slots]
        tokens_ref, cotangent_ref, left_ref = refs[slots : slots + 3]
        grad_ref, total_ref, scratch_ref = refs[-3:]
        step = pl.program_id(0)

        rows = got[0][...] if slots == 1 else jnp.concatenate([ref[...] for ref in got], axis=0)
        grad = dot(rows, left_ref[...], TN)
        grad_ref[...] = (cotangent_ref[...].astype(jnp.float32) + grad).astype(jnp.bfloat16)
        product = dot(rows, tokens_ref[...], NN)

        for block in range(own):
            part = product[:, block * order : (block + 1) * order]

            @pl.when(step == 0)
            def _():
                scratch_ref[block] = part

            @pl.when(step > 0)
            def _():
                scratch_ref[block] += part

        @pl.when(step == plan.steps - 1)
        def _():
            for block in range(own):
                part = scratch_ref[block, pl.ds(block, order, stride=own), :]
                total_ref[block] = part if chunk == 0 else part + refs[slots + 4][block]

    ins = (*received, tokens, cotangent, wide_left)
    in_specs = [*plan.slot_specs(), plan.token_spec(chunk), plan.token_spec(chunk), whole(wide_left)]
    aliases = {}
    if state is not None:
        aliases = {len(ins): 0, len(ins) + 1: 1}
        ins = (*ins, *state)
        in_specs += [pl.BlockSpec(memory_space=pl.ANY), whole(state[1])]
    outs = [
        jax.ShapeDtypeStruct(tokens.shape, jnp.bfloat16),
        jax.ShapeDtypeStruct((own, order, order), jnp.float32),
    ]
    out_specs = [plan.token_spec(chunk), whole(outs[1])]
    return call(
        body,
        plan,
        ins,
        in_specs,
        outs,
        out_specs,
        aliases,
        4 * plan.height * plan.width * plan.chunk,
        [pltpu.VMEM((own, plan.height, order), jnp.float32)],
    )


def exchange(plan, parts):
    if plan.direct:
        return [
            part if slot == 0 else lax.ppermute(part, "blk", [(i, i ^ slot) for i in range(plan.devices)])
            for slot, part in enumerate(parts)
        ]
    split = parts[0].reshape(plan.devices, plan.own * plan.own, plan.chunk)
    return [lax.all_to_all(split, "blk", 0, 0, tiled=True).reshape(plan.height, plan.chunk)]


def sum_over_dp(value):
    size = lax.axis_size("dp")
    if size == 2:
        return value.astype(jnp.float32) + lax.ppermute(value, "dp", [(0, 1), (1, 0)]).astype(jnp.float32)
    return lax.psum(value, "dp").astype(jnp.float32)


def local(tokens, left, right, cotangent, keep_mask, channel_order):
    rows, (own, order, _) = tokens.shape[0], left.shape
    devices = lax.axis_size("blk")
    plan = Plan(rows, own, order, devices)
    pair, pairs, span = plan.pair, plan.pairs, plan.pair * order
    partner = lax.iota(jnp.int32, devices)
    if plan.direct:
        partner = partner ^ lax.axis_index("blk")
    factor = 1.0 / math.sqrt(rows * lax.axis_size("dp"))

    selector = (channel_order[:, None] == lax.broadcasted_iota(jnp.int32, (order, order), 1)).astype(jnp.bfloat16)
    unpermuted_left = jnp.einsum("km,bko->obm", selector, left, preferred_element_type=jnp.float32).astype(jnp.bfloat16)
    slotted_left = jnp.take(unpermuted_left.reshape(devices, own, own, order), partner, axis=0)
    eye = jnp.eye(own, dtype=jnp.bfloat16)
    wide_left = (slotted_left.reshape(order, 1, own, order) * eye[None, :, :, None]).reshape(plan.height, plan.width)

    slotted_right = jnp.take(right.reshape(own, devices, own, order), partner, axis=1)
    slotted_right = slotted_right.reshape(pairs, pair, devices, own, order).transpose(0, 2, 1, 3, 4)
    eye_pair = jnp.eye(pair, dtype=jnp.bfloat16)
    wide_right = (slotted_right[:, :, :, :, None, :] * eye_pair[None, None, :, None, :, None]).reshape(
        pairs, pair * order, span
    )
    spread = jnp.repeat(eye, order, axis=1)

    forward = [
        exchange(plan, first_factor(plan, chunk, tokens, wide_left)) for chunk in range(plan.chunks)
    ]
    state, backward = None, []
    for chunk in range(plan.chunks):
        sent, state = second_factor(
            plan, chunk, forward[chunk], tokens, cotangent, keep_mask, spread, wide_right, state
        )
        backward.append(exchange(plan, sent))
    mixed, wide_total = state

    split_total = wide_total.reshape(pairs, devices, pair, own, pair, order)
    part_right = jnp.stack([split_total[:, :, jj, :, jj, :] for jj in range(pair)], axis=1)
    part_right = jnp.take(part_right.reshape(own, devices, own, order), partner, axis=1).reshape(own, order, order)
    grad_right = sum_over_dp(part_right.astype(jnp.bfloat16)) * factor

    state = None
    for chunk in range(plan.chunks):
        state = first_factor_back(plan, chunk, backward[chunk], tokens, cotangent, wide_left, state)
    grad_tokens, part_left = state
    part_left = jnp.take(part_left.astype(jnp.bfloat16).reshape(own, devices, own, order), partner, axis=1)
    part_left = jnp.einsum(
        "km,bom->bko", selector, part_left.reshape(own, order, order), preferred_element_type=jnp.float32
    ).astype(jnp.bfloat16)
    grad_left = sum_over_dp(part_left) * factor
    return (mixed, grad_tokens, grad_left, grad_right)


def solution(mesh):
    in_specs = (
        P("dp", "blk"),
        P("blk", None, None),
        P("blk", None, None),
        P("dp", "blk"),
        P("blk", "dp"),
        P(),
    )
    out_specs = (P("dp", "blk"), P("dp", "blk"), P("blk", None, None), P("blk", None, None))
    return jax.shard_map(local, mesh=mesh, in_specs=in_specs, out_specs=out_specs, check_vma=False)
```

```python
import math

import jax
import jax.numpy as jnp
import numpy as np
from jax import lax
from jax.experimental import pallas as pl
from jax.experimental.pallas import tpu as pltpu
from jax.sharding import PartitionSpec as P

keep_rate = 0.9
CHUNKS = 8
TILE = 512
VMEM_LIMIT = 60 * 1024 * 1024
FIRST_LAG = 4
SECOND_LAG = 2
ANY = pl.BlockSpec(memory_space=pl.ANY)
NT = (((1,), (1,)), ((), ()))
TN = (((0,), (0,)), ((), ()))
NN = (((1,), (0,)), ((), ()))


def dot(lhs, rhs, dims):
    return lax.dot_general(lhs, rhs, dims, preferred_element_type=jnp.float32)


class Plan:
    def __init__(self, rows, own, order, devices):
        self.rows, self.own, self.order, self.devices = rows, own, order, devices
        self.direct = (2 * own) % 16 == 0 and own >= 2
        self.pair = 2 if self.direct else own
        self.pairs = own // self.pair
        self.slots = devices if self.direct else 1
        quarter = max(devices // 4, 1)
        near, far = list(range(devices // 2)), list(range(devices // 2, devices))
        near = [hop for both in zip(near[:quarter], near[quarter:]) for hop in both]
        far = [hop for both in zip(far[:quarter], far[quarter:]) for hop in both]
        self.hops = [hop for both in zip(near, far) for hop in both]
        self.height = devices * own * own
        self.slot_height = self.height // self.slots
        self.width = own * order
        self.chunks = CHUNKS
        self.chunk = rows // self.chunks
        self.tile = math.gcd(self.chunk, TILE)
        self.steps = self.chunk // self.tile

    def token_spec(self, chunk):
        return pl.BlockSpec((self.tile, self.width), lambda i: (chunk * self.steps + i, 0))

    def slot_specs(self):
        return [pl.BlockSpec((self.slot_height, self.tile), lambda i: (0, i))] * self.slots

    def slot_shapes(self):
        return [jax.ShapeDtypeStruct((self.slot_height, self.chunk), jnp.bfloat16)] * self.slots

    def pair_rows(self, refs, pair):
        if self.pairs == 1 and self.slots == 1:
            return refs[0][...]
        size = self.pair * self.own
        return jnp.concatenate([ref[pair * size : (pair + 1) * size, :] for ref in refs], axis=0)


def whole(array):
    zeros = (0,) * array.ndim
    return pl.BlockSpec(array.shape, lambda i: zeros)


def call(body, plan, ins, in_specs, outs, out_specs, aliases, flops, scratch=()):
    size = sum(math.prod(o.shape) * o.dtype.itemsize for o in outs[: plan.slots]) * 4
    return pl.pallas_call(
        body,
        out_shape=outs,
        grid=(plan.steps,),
        in_specs=in_specs,
        out_specs=out_specs,
        scratch_shapes=scratch,
        input_output_aliases=aliases,
        compiler_params=pltpu.CompilerParams(vmem_limit_bytes=VMEM_LIMIT),
        cost_estimate=pl.CostEstimate(flops=flops, bytes_accessed=size, transcendentals=0),
    )(*ins)


def first_factor(plan, chunk, tokens, wide_left, after):
    def body(tokens_ref, left_ref, *refs):
        product = dot(left_ref[...], tokens_ref[...], NT).astype(jnp.bfloat16)
        for slot, ref in enumerate(refs[len(after) :]):
            ref[...] = product[slot * plan.slot_height : (slot + 1) * plan.slot_height, :]

    return call(
        body,
        plan,
        (tokens, wide_left, *after),
        [plan.token_spec(chunk), whole(wide_left), *[ANY] * len(after)],
        plan.slot_shapes(),
        plan.slot_specs(),
        {},
        2 * plan.height * plan.width * plan.chunk,
    )


def second_factor(plan, chunk, received, tokens, cotangent, keep_mask, spread, wide_right, state, after):
    slots, span = plan.slots, plan.pair * plan.order

    def body(*refs):
        got = refs[:slots]
        tokens_ref, cotangent_ref, mask_ref, spread_ref, right_ref = refs[slots : slots + 5]
        outs = refs[len(refs) - slots - 2 :]
        sent, mixed_ref, total_ref = outs[:slots], outs[slots], outs[slots + 1]

        @pl.when(pl.program_id(0) == 0)
        def _():
            if chunk == 0:
                total_ref[...] = jnp.zeros_like(total_ref)
            else:
                total_ref[...] = refs[slots + 6][...]

        mask = mask_ref[...].astype(jnp.float32).astype(jnp.bfloat16)
        for pair in range(plan.pairs):
            columns = slice(pair * span, (pair + 1) * span)
            kept = dot(mask, spread_ref[:, columns], TN) * jnp.float32(1.0 / keep_rate)
            rows = plan.pair_rows(got, pair)
            mixing = dot(rows, right_ref[pair], TN)
            cdf = 0.5 * (1.0 + lax.erf(mixing * jnp.float32(1.0 / math.sqrt(2.0))))
            pdf = jnp.exp(-0.5 * mixing * mixing) * jnp.float32(1.0 / math.sqrt(2.0 * math.pi))
            branch = kept * mixing * cdf
            mixed_ref[:, columns] = (tokens_ref[:, columns].astype(jnp.float32) + branch).astype(jnp.bfloat16)
            grad_mix = (cotangent_ref[:, columns].astype(jnp.float32) * kept * (cdf + mixing * pdf)).astype(
                jnp.bfloat16
            )
            total_ref[pair] += dot(rows, grad_mix, NN)
            back = dot(right_ref[pair], grad_mix, NT).astype(jnp.bfloat16)
            if plan.pairs == 1 and slots == 1:
                sent[0][...] = back
            else:
                size = plan.pair * plan.own
                for slot, ref in enumerate(sent):
                    ref[pair * size : (pair + 1) * size, :] = back[slot * size : (slot + 1) * size, :]

    ins = (*received, tokens, cotangent, keep_mask, spread, wide_right)
    in_specs = [
        *plan.slot_specs(),
        plan.token_spec(chunk),
        plan.token_spec(chunk),
        pl.BlockSpec((plan.own, plan.tile), lambda i: (0, chunk * plan.steps + i)),
        whole(spread),
        whole(wide_right),
    ]
    aliases = {}
    if state is not None:
        aliases = {len(ins): slots, len(ins) + 1: slots + 1}
        ins = (*ins, *state)
        in_specs += [ANY, whole(state[1])]
    ins = (*ins, *after)
    in_specs += [ANY] * len(after)
    outs = [
        *plan.slot_shapes(),
        jax.ShapeDtypeStruct(tokens.shape, jnp.bfloat16),
        jax.ShapeDtypeStruct((plan.pairs, plan.pair * plan.order, span), jnp.float32),
    ]
    out_specs = [*plan.slot_specs(), plan.token_spec(chunk), whole(outs[-1])]
    flops = 6 * plan.height * span * plan.chunk * 4
    result = call(body, plan, ins, in_specs, outs, out_specs, aliases, flops)
    return result[:slots], (result[slots], result[slots + 1])


def first_factor_back(plan, chunk, received, tokens, cotangent, wide_left, state):
    slots, own, order = plan.slots, plan.own, plan.order

    def body(*refs):
        got = refs[:slots]
        tokens_ref, cotangent_ref, left_ref = refs[slots : slots + 3]
        grad_ref, total_ref, scratch_ref = refs[-3:]
        step = pl.program_id(0)

        rows = got[0][...] if slots == 1 else jnp.concatenate([ref[...] for ref in got], axis=0)
        grad = dot(rows, left_ref[...], TN)
        grad_ref[...] = (cotangent_ref[...].astype(jnp.float32) + grad).astype(jnp.bfloat16)
        product = dot(rows, tokens_ref[...], NN)

        for block in range(own):
            part = product[:, block * order : (block + 1) * order]

            @pl.when(step == 0)
            def _():
                scratch_ref[block] = part

            @pl.when(step > 0)
            def _():
                scratch_ref[block] += part

        @pl.when(step == plan.steps - 1)
        def _():
            for block in range(own):
                part = scratch_ref[block, pl.ds(block, order, stride=own), :]
                total_ref[block] = part if chunk == 0 else part + refs[slots + 4][block]

    ins = (*received, tokens, cotangent, wide_left)
    in_specs = [*plan.slot_specs(), plan.token_spec(chunk), plan.token_spec(chunk), whole(wide_left)]
    aliases = {}
    if state is not None:
        aliases = {len(ins): 0, len(ins) + 1: 1}
        ins = (*ins, *state)
        in_specs += [ANY, whole(state[1])]
    outs = [
        jax.ShapeDtypeStruct(tokens.shape, jnp.bfloat16),
        jax.ShapeDtypeStruct((own, order, order), jnp.float32),
    ]
    out_specs = [plan.token_spec(chunk), whole(outs[1])]
    return call(
        body,
        plan,
        ins,
        in_specs,
        outs,
        out_specs,
        aliases,
        4 * plan.height * plan.width * plan.chunk,
        [pltpu.VMEM((own, plan.height, order), jnp.float32)],
    )


def exchange(plan, parts):
    if plan.direct:
        return [
            part if hop == 0 else lax.ppermute(part, "blk", [(i, i ^ hop) for i in range(plan.devices)])
            for hop, part in zip(plan.hops, parts)
        ]
    split = parts[0].reshape(plan.devices, plan.own * plan.own, plan.chunk)
    return [lax.all_to_all(split, "blk", 0, 0, tiled=True).reshape(plan.height, plan.chunk)]


def sum_over_dp(value):
    size = lax.axis_size("dp")
    if size == 2:
        return value.astype(jnp.float32) + lax.ppermute(value, "dp", [(0, 1), (1, 0)]).astype(jnp.float32)
    return lax.psum(value, "dp").astype(jnp.float32)


def local(tokens, left, right, cotangent, keep_mask, channel_order):
    rows, (own, order, _) = tokens.shape[0], left.shape
    devices = lax.axis_size("blk")
    plan = Plan(rows, own, order, devices)
    pair, pairs, span = plan.pair, plan.pairs, plan.pair * order
    partner = place = lax.iota(jnp.int32, devices)
    if plan.direct:
        place = jnp.take(jnp.array(np.argsort(plan.hops), jnp.int32), place ^ lax.axis_index("blk"))
        partner = jnp.array(plan.hops, jnp.int32) ^ lax.axis_index("blk")
    factor = 1.0 / math.sqrt(rows * lax.axis_size("dp"))

    selector = (channel_order[:, None] == lax.broadcasted_iota(jnp.int32, (order, order), 1)).astype(jnp.bfloat16)
    unpermuted_left = jnp.einsum("km,bko->obm", selector, left, preferred_element_type=jnp.float32).astype(jnp.bfloat16)
    slotted_left = jnp.take(unpermuted_left.reshape(devices, own, own, order), partner, axis=0)
    eye = jnp.eye(own, dtype=jnp.bfloat16)
    wide_left = (slotted_left.reshape(order, 1, own, order) * eye[None, :, :, None]).reshape(plan.height, plan.width)

    slotted_right = jnp.take(right.reshape(own, devices, own, order), partner, axis=1)
    slotted_right = slotted_right.reshape(pairs, pair, devices, own, order).transpose(0, 2, 1, 3, 4)
    eye_pair = jnp.eye(pair, dtype=jnp.bfloat16)
    wide_right = (slotted_right[:, :, :, :, None, :] * eye_pair[None, None, :, None, :, None]).reshape(
        pairs, pair * order, span
    )
    spread = jnp.repeat(eye, order, axis=1)

    forward, backward, state = [], [], None
    for step in range(plan.chunks + SECOND_LAG):
        if step < plan.chunks:
            after = backward[step - FIRST_LAG][1:] if step >= FIRST_LAG else []
            forward.append(exchange(plan, first_factor(plan, step, tokens, wide_left, after)))
        chunk = step - SECOND_LAG
        if chunk >= 0:
            after = backward[chunk - SECOND_LAG][1:] if chunk >= SECOND_LAG else []
            sent, state = second_factor(
                plan, chunk, forward[chunk], tokens, cotangent, keep_mask, spread, wide_right, state, after
            )
            backward.append(exchange(plan, sent))
    mixed, wide_total = state

    split_total = wide_total.reshape(pairs, devices, pair, own, pair, order)
    part_right = jnp.stack([split_total[:, :, jj, :, jj, :] for jj in range(pair)], axis=1)
    part_right = jnp.take(part_right.reshape(own, devices, own, order), place, axis=1).reshape(own, order, order)
    grad_right = sum_over_dp(part_right.astype(jnp.bfloat16)) * factor

    state = None
    for chunk in range(plan.chunks):
        state = first_factor_back(plan, chunk, backward[chunk], tokens, cotangent, wide_left, state)
    grad_tokens, part_left = state
    part_left = jnp.take(part_left.astype(jnp.bfloat16).reshape(own, devices, own, order), place, axis=1)
    part_left = jnp.einsum(
        "km,bom->bko", selector, part_left.reshape(own, order, order), preferred_element_type=jnp.float32
    ).astype(jnp.bfloat16)
    grad_left = sum_over_dp(part_left) * factor
    return (mixed, grad_tokens, grad_left, grad_right)


def solution(mesh):
    in_specs = (
        P("dp", "blk"),
        P("blk", None, None),
        P("blk", None, None),
        P("dp", "blk"),
        P("blk", "dp"),
        P(),
    )
    out_specs = (P("dp", "blk"), P("dp", "blk"), P("blk", None, None), P("blk", None, None))
    return jax.shard_map(local, mesh=mesh, in_specs=in_specs, out_specs=out_specs, check_vma=False)
```

```python
import math

import jax
import jax.numpy as jnp
import numpy as np
from jax import lax
from jax.experimental import pallas as pl
from jax.experimental.pallas import tpu as pltpu
from jax.sharding import PartitionSpec as P

keep_rate = 0.9
CHUNKS = 8
TILE = 512
VMEM_LIMIT = 60 * 1024 * 1024
FIRST_LAG = 4
SECOND_LAG = 2
ANY = pl.BlockSpec(memory_space=pl.ANY)
NT = (((1,), (1,)), ((), ()))
TN = (((0,), (0,)), ((), ()))
NN = (((1,), (0,)), ((), ()))


def dot(lhs, rhs, dims):
    return lax.dot_general(lhs, rhs, dims, preferred_element_type=jnp.float32)


class Plan:
    def __init__(self, rows, own, order, devices):
        self.rows, self.own, self.order, self.devices = rows, own, order, devices
        self.direct = (2 * own) % 16 == 0 and own >= 2
        self.pair = 2 if self.direct else own
        self.pairs = own // self.pair
        self.height = devices * own * own
        self.near = devices // 2 if self.direct else devices
        far = list(range(self.near, devices))
        self.hops = [hop for both in zip(far[: len(far) // 2], far[len(far) // 2 :]) for hop in both]
        self.heights = [self.near * own * own] + [own * own] * len(self.hops)
        self.slots = len(self.heights)
        self.width = own * order
        self.chunks = CHUNKS
        self.chunk = rows // self.chunks
        self.tile = math.gcd(self.chunk, TILE)
        self.steps = self.chunk // self.tile

    def token_spec(self, chunk):
        return pl.BlockSpec((self.tile, self.width), lambda i: (chunk * self.steps + i, 0))

    def slot_specs(self):
        return [pl.BlockSpec((height, self.tile), lambda i: (0, i)) for height in self.heights]

    def slot_shapes(self):
        return [jax.ShapeDtypeStruct((height, self.chunk), jnp.bfloat16) for height in self.heights]

    def pieces(self, refs, pair):
        size, step = self.pair * self.own, self.own * self.own
        for device in range(self.near):
            start = device * step + pair * size
            yield refs[0], slice(start, start + size)
        for ref in refs[1:]:
            yield ref, slice(pair * size, (pair + 1) * size)


def whole(array):
    zeros = (0,) * array.ndim
    return pl.BlockSpec(array.shape, lambda i: zeros)


def call(body, plan, ins, in_specs, outs, out_specs, aliases, flops, scratch=()):
    size = sum(math.prod(o.shape) * o.dtype.itemsize for o in outs[: plan.slots]) * 4
    return pl.pallas_call(
        body,
        out_shape=outs,
        grid=(plan.steps,),
        in_specs=in_specs,
        out_specs=out_specs,
        scratch_shapes=scratch,
        input_output_aliases=aliases,
        compiler_params=pltpu.CompilerParams(vmem_limit_bytes=VMEM_LIMIT),
        cost_estimate=pl.CostEstimate(flops=flops, bytes_accessed=size, transcendentals=0),
    )(*ins)


def first_factor(plan, chunk, tokens, wide_left, after):
    def body(tokens_ref, left_ref, *refs):
        product = dot(left_ref[...], tokens_ref[...], NT).astype(jnp.bfloat16)
        start = 0
        for ref in refs[len(after) :]:
            ref[...] = product[start : start + ref.shape[0], :]
            start += ref.shape[0]

    return call(
        body,
        plan,
        (tokens, wide_left, *after),
        [plan.token_spec(chunk), whole(wide_left), *[ANY] * len(after)],
        plan.slot_shapes(),
        plan.slot_specs(),
        {},
        2 * plan.height * plan.width * plan.chunk,
    )


def second_factor(plan, chunk, received, tokens, cotangent, keep_mask, spread, wide_right, state, after):
    slots, span = plan.slots, plan.pair * plan.order

    def body(*refs):
        got = refs[:slots]
        tokens_ref, cotangent_ref, mask_ref, spread_ref, right_ref = refs[slots : slots + 5]
        outs = refs[len(refs) - slots - 2 :]
        sent, mixed_ref, total_ref = outs[:slots], outs[slots], outs[slots + 1]

        @pl.when(pl.program_id(0) == 0)
        def _():
            if chunk == 0:
                total_ref[...] = jnp.zeros_like(total_ref)
            else:
                total_ref[...] = refs[slots + 6][...]

        mask = mask_ref[...].astype(jnp.float32).astype(jnp.bfloat16)
        for pair in range(plan.pairs):
            columns = slice(pair * span, (pair + 1) * span)
            kept = dot(mask, spread_ref[:, columns], TN) * jnp.float32(1.0 / keep_rate)
            rows = got[0][...]
            if plan.direct:
                rows = jnp.concatenate([ref[piece, :] for ref, piece in plan.pieces(got, pair)], axis=0)
            mixing = dot(rows, right_ref[pair], TN)
            cdf = 0.5 * (1.0 + lax.erf(mixing * jnp.float32(1.0 / math.sqrt(2.0))))
            pdf = jnp.exp(-0.5 * mixing * mixing) * jnp.float32(1.0 / math.sqrt(2.0 * math.pi))
            branch = kept * mixing * cdf
            mixed_ref[:, columns] = (tokens_ref[:, columns].astype(jnp.float32) + branch).astype(jnp.bfloat16)
            grad_mix = (cotangent_ref[:, columns].astype(jnp.float32) * kept * (cdf + mixing * pdf)).astype(
                jnp.bfloat16
            )
            total_ref[pair] += dot(rows, grad_mix, NN)
            back = dot(right_ref[pair], grad_mix, NT).astype(jnp.bfloat16)
            if plan.direct:
                size = plan.pair * plan.own
                for device, (ref, piece) in enumerate(plan.pieces(sent, pair)):
                    ref[piece, :] = back[device * size : (device + 1) * size, :]
            else:
                sent[0][...] = back

    ins = (*received, tokens, cotangent, keep_mask, spread, wide_right)
    in_specs = [
        *plan.slot_specs(),
        plan.token_spec(chunk),
        plan.token_spec(chunk),
        pl.BlockSpec((plan.own, plan.tile), lambda i: (0, chunk * plan.steps + i)),
        whole(spread),
        whole(wide_right),
    ]
    aliases = {}
    if state is not None:
        aliases = {len(ins): slots, len(ins) + 1: slots + 1}
        ins = (*ins, *state)
        in_specs += [ANY, whole(state[1])]
    ins = (*ins, *after)
    in_specs += [ANY] * len(after)
    outs = [
        *plan.slot_shapes(),
        jax.ShapeDtypeStruct(tokens.shape, jnp.bfloat16),
        jax.ShapeDtypeStruct((plan.pairs, plan.pair * plan.order, span), jnp.float32),
    ]
    out_specs = [*plan.slot_specs(), plan.token_spec(chunk), whole(outs[-1])]
    flops = 6 * plan.height * span * plan.chunk * 4
    result = call(body, plan, ins, in_specs, outs, out_specs, aliases, flops)
    return result[:slots], (result[slots], result[slots + 1])


def tokens_back(plan, chunk, received, cotangent, wide_left, grad_tokens):
    slots = plan.slots

    def body(*refs):
        got, (cotangent_ref, left_ref), grad_ref = refs[:slots], refs[slots : slots + 2], refs[-1]
        rows = jnp.concatenate([ref[...] for ref in got], axis=0) if slots > 1 else got[0][...]
        grad = dot(rows, left_ref[...], TN)
        grad_ref[...] = (cotangent_ref[...].astype(jnp.float32) + grad).astype(jnp.bfloat16)

    ins = (*received, cotangent, wide_left)
    in_specs = [*plan.slot_specs(), plan.token_spec(chunk), whole(wide_left)]
    aliases = {}
    if grad_tokens is not None:
        aliases = {len(ins): 0}
        ins = (*ins, grad_tokens)
        in_specs.append(ANY)
    outs = [jax.ShapeDtypeStruct(cotangent.shape, jnp.bfloat16)]
    flops = 2 * plan.height * plan.width * plan.chunk
    return call(body, plan, ins, in_specs, outs, [plan.token_spec(chunk)], aliases, flops)[0]


def left_back(plan, chunk, received, tokens, total):
    slots, own, order = plan.slots, plan.own, plan.order

    def body(*refs):
        got, tokens_ref = refs[:slots], refs[slots]
        total_ref, scratch_ref = refs[-2:]
        step = pl.program_id(0)
        rows = jnp.concatenate([ref[...] for ref in got], axis=0) if slots > 1 else got[0][...]
        product = dot(rows, tokens_ref[...], NN)
        for block in range(own):
            part = product[:, block * order : (block + 1) * order]

            @pl.when(step == 0)
            def _():
                scratch_ref[block] = part

            @pl.when(step > 0)
            def _():
                scratch_ref[block] += part

        @pl.when(step == plan.steps - 1)
        def _():
            for block in range(own):
                part = scratch_ref[block, pl.ds(block, order, stride=own), :]
                total_ref[block] = part if total is None else part + refs[slots + 1][block]

    ins = (*received, tokens)
    in_specs = [*plan.slot_specs(), plan.token_spec(chunk)]
    if total is not None:
        ins = (*ins, total)
        in_specs.append(whole(total))
    outs = [jax.ShapeDtypeStruct((own, order, order), jnp.float32)]
    scratch = [pltpu.VMEM((own, plan.height, order), jnp.float32)]
    flops = 2 * plan.height * plan.width * plan.chunk
    return call(body, plan, ins, in_specs, outs, [whole(outs[0])], {}, flops, scratch)[0]


def exchange(plan, parts):
    devices, near = plan.devices, plan.near
    far = [
        lax.ppermute(part, "blk", [(i, i ^ hop) for i in range(devices)]) for hop, part in zip(plan.hops, parts[1:])
    ]
    groups = [list(range(start, start + near)) for start in range(0, devices, near)]
    split = parts[0].reshape(near, plan.own * plan.own, plan.chunk)
    got = lax.all_to_all(split, "blk", 0, 0, axis_index_groups=groups, tiled=True)
    return [got.reshape(parts[0].shape), *far]


def sum_over_dp(value):
    size = lax.axis_size("dp")
    if size == 2:
        return value.astype(jnp.float32) + lax.ppermute(value, "dp", [(0, 1), (1, 0)]).astype(jnp.float32)
    return lax.psum(value, "dp").astype(jnp.float32)


def local(tokens, left, right, cotangent, keep_mask, channel_order):
    rows, (own, order, _) = tokens.shape[0], left.shape
    devices = lax.axis_size("blk")
    plan = Plan(rows, own, order, devices)
    pair, pairs, span = plan.pair, plan.pairs, plan.pair * order
    partner = place = lax.iota(jnp.int32, devices)
    if plan.direct:
        me, near = lax.axis_index("blk"), plan.near
        hops = place ^ me
        far_place = near + jnp.array(np.argsort(plan.hops), jnp.int32)
        place = jnp.where(hops < near, place % near, jnp.take(far_place, hops % near))
        partner = jnp.concatenate(
            [me // near * near + lax.iota(jnp.int32, near), jnp.array(plan.hops, jnp.int32) ^ me]
        )
    factor = 1.0 / math.sqrt(rows * lax.axis_size("dp"))

    selector = (channel_order[:, None] == lax.broadcasted_iota(jnp.int32, (order, order), 1)).astype(jnp.bfloat16)
    unpermuted_left = jnp.einsum("km,bko->obm", selector, left, preferred_element_type=jnp.float32).astype(jnp.bfloat16)
    slotted_left = jnp.take(unpermuted_left.reshape(devices, own, own, order), partner, axis=0)
    eye = jnp.eye(own, dtype=jnp.bfloat16)
    wide_left = (slotted_left.reshape(order, 1, own, order) * eye[None, :, :, None]).reshape(plan.height, plan.width)

    slotted_right = jnp.take(right.reshape(own, devices, own, order), partner, axis=1)
    slotted_right = slotted_right.reshape(pairs, pair, devices, own, order).transpose(0, 2, 1, 3, 4)
    eye_pair = jnp.eye(pair, dtype=jnp.bfloat16)
    wide_right = (slotted_right[:, :, :, :, None, :] * eye_pair[None, None, :, None, :, None]).reshape(
        pairs, pair * order, span
    )
    spread = jnp.repeat(eye, order, axis=1)

    forward, backward, state = [], [], None
    for step in range(plan.chunks + SECOND_LAG):
        if step < plan.chunks:
            after = backward[step - FIRST_LAG] if step >= FIRST_LAG else []
            forward.append(exchange(plan, first_factor(plan, step, tokens, wide_left, after)))
        chunk = step - SECOND_LAG
        if chunk >= 0:
            after = backward[chunk - SECOND_LAG] if chunk >= SECOND_LAG else []
            sent, state = second_factor(
                plan, chunk, forward[chunk], tokens, cotangent, keep_mask, spread, wide_right, state, after
            )
            backward.append(exchange(plan, sent))
    mixed, wide_total = state

    split_total = wide_total.reshape(pairs, devices, pair, own, pair, order)
    part_right = jnp.stack([split_total[:, :, jj, :, jj, :] for jj in range(pair)], axis=1)
    part_right = jnp.take(part_right.reshape(own, devices, own, order), place, axis=1).reshape(own, order, order)
    grad_right = sum_over_dp(part_right.astype(jnp.bfloat16)) * factor

    grad_tokens = part_left = None
    for chunk in range(plan.chunks):
        part_left = left_back(plan, chunk, backward[chunk], tokens, part_left)
        grad_tokens = tokens_back(plan, chunk, backward[chunk], cotangent, wide_left, grad_tokens)
    part_left = jnp.take(part_left.astype(jnp.bfloat16).reshape(own, devices, own, order), place, axis=1)
    part_left = jnp.einsum(
        "km,bom->bko", selector, part_left.reshape(own, order, order), preferred_element_type=jnp.float32
    ).astype(jnp.bfloat16)
    grad_left = sum_over_dp(part_left) * factor
    return (mixed, grad_tokens, grad_left, grad_right)


def solution(mesh):
    in_specs = (
        P("dp", "blk"),
        P("blk", None, None),
        P("blk", None, None),
        P("dp", "blk"),
        P("blk", "dp"),
        P(),
    )
    out_specs = (P("dp", "blk"), P("dp", "blk"), P("blk", None, None), P("blk", None, None))
    return jax.shard_map(local, mesh=mesh, in_specs=in_specs, out_specs=out_specs, check_vma=False)
```

```python
import math

import jax
import jax.numpy as jnp
import numpy as np
from jax import lax
from jax.experimental import pallas as pl
from jax.experimental.pallas import tpu as pltpu
from jax.sharding import PartitionSpec as P

keep_rate = 0.9
CHUNKS = 6
TILE = 512
VMEM_LIMIT = 60 * 1024 * 1024
FIRST_LAG = 4
SECOND_LAG = 2
ANY = pl.BlockSpec(memory_space=pl.ANY)
NT = (((1,), (1,)), ((), ()))
TN = (((0,), (0,)), ((), ()))
NN = (((1,), (0,)), ((), ()))


def dot(lhs, rhs, dims):
    return lax.dot_general(lhs, rhs, dims, preferred_element_type=jnp.float32)


class Plan:
    def __init__(self, rows, own, order, devices):
        self.rows, self.own, self.order, self.devices = rows, own, order, devices
        self.direct = (2 * own) % 16 == 0 and own >= 2
        self.pair = 2 if self.direct else own
        self.pairs = own // self.pair
        self.slots = devices if self.direct else 1
        quarter = max(devices // 4, 1)
        near, far = list(range(devices // 2)), list(range(devices // 2, devices))
        near = [hop for both in zip(near[:quarter], near[quarter:]) for hop in both]
        far = [hop for both in zip(far[:quarter], far[quarter:]) for hop in both]
        self.hops = [hop for both in zip(near, far) for hop in both]
        self.height = devices * own * own
        self.slot_height = self.height // self.slots
        self.width = own * order
        self.chunks = CHUNKS
        self.chunk = rows // self.chunks
        self.tile = math.gcd(self.chunk, TILE)
        self.steps = self.chunk // self.tile

    def token_spec(self, chunk):
        return pl.BlockSpec((self.tile, self.width), lambda i: (chunk * self.steps + i, 0))

    def slot_specs(self):
        return [pl.BlockSpec((self.slot_height, self.tile), lambda i: (0, i))] * self.slots

    def slot_shapes(self):
        return [jax.ShapeDtypeStruct((self.slot_height, self.chunk), jnp.bfloat16)] * self.slots

    def pair_rows(self, refs, pair):
        if self.pairs == 1 and self.slots == 1:
            return refs[0][...]
        size = self.pair * self.own
        return jnp.concatenate([ref[pair * size : (pair + 1) * size, :] for ref in refs], axis=0)


def whole(array):
    zeros = (0,) * array.ndim
    return pl.BlockSpec(array.shape, lambda i: zeros)


def call(body, plan, ins, in_specs, outs, out_specs, aliases, flops, scratch=()):
    size = sum(math.prod(o.shape) * o.dtype.itemsize for o in outs[: plan.slots]) * 4
    return pl.pallas_call(
        body,
        out_shape=outs,
        grid=(plan.steps,),
        in_specs=in_specs,
        out_specs=out_specs,
        scratch_shapes=scratch,
        input_output_aliases=aliases,
        compiler_params=pltpu.CompilerParams(vmem_limit_bytes=VMEM_LIMIT),
        cost_estimate=pl.CostEstimate(flops=flops, bytes_accessed=size, transcendentals=0),
    )(*ins)


def first_factor(plan, chunk, tokens, wide_left, after):
    def body(tokens_ref, left_ref, *refs):
        product = dot(left_ref[...], tokens_ref[...], NT).astype(jnp.bfloat16)
        for slot, ref in enumerate(refs[len(after) :]):
            ref[...] = product[slot * plan.slot_height : (slot + 1) * plan.slot_height, :]

    return call(
        body,
        plan,
        (tokens, wide_left, *after),
        [plan.token_spec(chunk), whole(wide_left), *[ANY] * len(after)],
        plan.slot_shapes(),
        plan.slot_specs(),
        {},
        2 * plan.height * plan.width * plan.chunk,
    )


def second_factor(plan, chunk, received, tokens, cotangent, keep_mask, spread, wide_right, state, after):
    slots, span = plan.slots, plan.pair * plan.order

    def body(*refs):
        got = refs[:slots]
        tokens_ref, cotangent_ref, mask_ref, spread_ref, right_ref = refs[slots : slots + 5]
        outs = refs[len(refs) - slots - 2 :]
        sent, mixed_ref, total_ref = outs[:slots], outs[slots], outs[slots + 1]

        @pl.when(pl.program_id(0) == 0)
        def _():
            if chunk == 0:
                total_ref[...] = jnp.zeros_like(total_ref)
            else:
                total_ref[...] = refs[slots + 6][...]

        mask = mask_ref[...].astype(jnp.float32).astype(jnp.bfloat16)
        for pair in range(plan.pairs):
            columns = slice(pair * span, (pair + 1) * span)
            kept = dot(mask, spread_ref[:, columns], TN) * jnp.float32(1.0 / keep_rate)
            rows = plan.pair_rows(got, pair)
            mixing = dot(rows, right_ref[pair], TN)
            cdf = 0.5 * (1.0 + lax.erf(mixing * jnp.float32(1.0 / math.sqrt(2.0))))
            pdf = jnp.exp(-0.5 * mixing * mixing) * jnp.float32(1.0 / math.sqrt(2.0 * math.pi))
            branch = kept * mixing * cdf
            mixed_ref[:, columns] = (tokens_ref[:, columns].astype(jnp.float32) + branch).astype(jnp.bfloat16)
            grad_mix = (cotangent_ref[:, columns].astype(jnp.float32) * kept * (cdf + mixing * pdf)).astype(
                jnp.bfloat16
            )
            total_ref[pair] += dot(rows, grad_mix, NN)
            back = dot(right_ref[pair], grad_mix, NT).astype(jnp.bfloat16)
            if plan.pairs == 1 and slots == 1:
                sent[0][...] = back
            else:
                size = plan.pair * plan.own
                for slot, ref in enumerate(sent):
                    ref[pair * size : (pair + 1) * size, :] = back[slot * size : (slot + 1) * size, :]

    ins = (*received, tokens, cotangent, keep_mask, spread, wide_right)
    in_specs = [
        *plan.slot_specs(),
        plan.token_spec(chunk),
        plan.token_spec(chunk),
        pl.BlockSpec((plan.own, plan.tile), lambda i: (0, chunk * plan.steps + i)),
        whole(spread),
        whole(wide_right),
    ]
    aliases = {}
    if state is not None:
        aliases = {len(ins): slots, len(ins) + 1: slots + 1}
        ins = (*ins, *state)
        in_specs += [ANY, whole(state[1])]
    ins = (*ins, *after)
    in_specs += [ANY] * len(after)
    outs = [
        *plan.slot_shapes(),
        jax.ShapeDtypeStruct(tokens.shape, jnp.bfloat16),
        jax.ShapeDtypeStruct((plan.pairs, plan.pair * plan.order, span), jnp.float32),
    ]
    out_specs = [*plan.slot_specs(), plan.token_spec(chunk), whole(outs[-1])]
    flops = 6 * plan.height * span * plan.chunk * 4
    result = call(body, plan, ins, in_specs, outs, out_specs, aliases, flops)
    return result[:slots], (result[slots], result[slots + 1])


def first_factor_back(plan, chunk, received, tokens, cotangent, wide_left, state):
    slots, own, order = plan.slots, plan.own, plan.order

    def body(*refs):
        got = refs[:slots]
        tokens_ref, cotangent_ref, left_ref = refs[slots : slots + 3]
        grad_ref, total_ref, scratch_ref = refs[-3:]
        step = pl.program_id(0)

        rows = got[0][...] if slots == 1 else jnp.concatenate([ref[...] for ref in got], axis=0)
        grad = dot(rows, left_ref[...], TN)
        grad_ref[...] = (cotangent_ref[...].astype(jnp.float32) + grad).astype(jnp.bfloat16)
        product = dot(rows, tokens_ref[...], NN)

        for block in range(own):
            part = product[:, block * order : (block + 1) * order]

            @pl.when(step == 0)
            def _():
                scratch_ref[block] = part

            @pl.when(step > 0)
            def _():
                scratch_ref[block] += part

        @pl.when(step == plan.steps - 1)
        def _():
            for block in range(own):
                part = scratch_ref[block, pl.ds(block, order, stride=own), :]
                total_ref[block] = part if chunk == 0 else part + refs[slots + 4][block]

    ins = (*received, tokens, cotangent, wide_left)
    in_specs = [*plan.slot_specs(), plan.token_spec(chunk), plan.token_spec(chunk), whole(wide_left)]
    aliases = {}
    if state is not None:
        aliases = {len(ins): 0, len(ins) + 1: 1}
        ins = (*ins, *state)
        in_specs += [ANY, whole(state[1])]
    outs = [
        jax.ShapeDtypeStruct(tokens.shape, jnp.bfloat16),
        jax.ShapeDtypeStruct((own, order, order), jnp.float32),
    ]
    out_specs = [plan.token_spec(chunk), whole(outs[1])]
    return call(
        body,
        plan,
        ins,
        in_specs,
        outs,
        out_specs,
        aliases,
        4 * plan.height * plan.width * plan.chunk,
        [pltpu.VMEM((own, plan.height, order), jnp.float32)],
    )


def exchange(plan, parts):
    if plan.direct:
        return [
            part if hop == 0 else lax.ppermute(part, "blk", [(i, i ^ hop) for i in range(plan.devices)])
            for hop, part in zip(plan.hops, parts)
        ]
    split = parts[0].reshape(plan.devices, plan.own * plan.own, plan.chunk)
    return [lax.all_to_all(split, "blk", 0, 0, tiled=True).reshape(plan.height, plan.chunk)]


def sum_over_dp(value):
    size = lax.axis_size("dp")
    if size == 2:
        return value.astype(jnp.float32) + lax.ppermute(value, "dp", [(0, 1), (1, 0)]).astype(jnp.float32)
    return lax.psum(value, "dp").astype(jnp.float32)


def local(tokens, left, right, cotangent, keep_mask, channel_order):
    rows, (own, order, _) = tokens.shape[0], left.shape
    devices = lax.axis_size("blk")
    plan = Plan(rows, own, order, devices)
    pair, pairs, span = plan.pair, plan.pairs, plan.pair * order
    partner = place = lax.iota(jnp.int32, devices)
    if plan.direct:
        place = jnp.take(jnp.array(np.argsort(plan.hops), jnp.int32), place ^ lax.axis_index("blk"))
        partner = jnp.array(plan.hops, jnp.int32) ^ lax.axis_index("blk")
    factor = 1.0 / math.sqrt(rows * lax.axis_size("dp"))

    selector = (channel_order[:, None] == lax.broadcasted_iota(jnp.int32, (order, order), 1)).astype(jnp.bfloat16)
    unpermuted_left = jnp.einsum("km,bko->obm", selector, left, preferred_element_type=jnp.float32).astype(jnp.bfloat16)
    slotted_left = jnp.take(unpermuted_left.reshape(devices, own, own, order), partner, axis=0)
    eye = jnp.eye(own, dtype=jnp.bfloat16)
    wide_left = (slotted_left.reshape(order, 1, own, order) * eye[None, :, :, None]).reshape(plan.height, plan.width)

    slotted_right = jnp.take(right.reshape(own, devices, own, order), partner, axis=1)
    slotted_right = slotted_right.reshape(pairs, pair, devices, own, order).transpose(0, 2, 1, 3, 4)
    eye_pair = jnp.eye(pair, dtype=jnp.bfloat16)
    wide_right = (slotted_right[:, :, :, :, None, :] * eye_pair[None, None, :, None, :, None]).reshape(
        pairs, pair * order, span
    )
    spread = jnp.repeat(eye, order, axis=1)

    forward, backward, state = [], [], None
    for step in range(plan.chunks + SECOND_LAG):
        if step < plan.chunks:
            after = backward[step - FIRST_LAG][1:] if step >= FIRST_LAG else []
            forward.append(exchange(plan, first_factor(plan, step, tokens, wide_left, after)))
        chunk = step - SECOND_LAG
        if chunk >= 0:
            after = backward[chunk - SECOND_LAG][1:] if chunk >= SECOND_LAG else []
            sent, state = second_factor(
                plan, chunk, forward[chunk], tokens, cotangent, keep_mask, spread, wide_right, state, after
            )
            backward.append(exchange(plan, sent))
    mixed, wide_total = state

    split_total = wide_total.reshape(pairs, devices, pair, own, pair, order)
    part_right = jnp.stack([split_total[:, :, jj, :, jj, :] for jj in range(pair)], axis=1)
    part_right = jnp.take(part_right.reshape(own, devices, own, order), place, axis=1).reshape(own, order, order)
    grad_right = sum_over_dp(part_right.astype(jnp.bfloat16)) * factor

    state = None
    for chunk in range(plan.chunks):
        state = first_factor_back(plan, chunk, backward[chunk], tokens, cotangent, wide_left, state)
    grad_tokens, part_left = state
    part_left = jnp.take(part_left.astype(jnp.bfloat16).reshape(own, devices, own, order), place, axis=1)
    part_left = jnp.einsum(
        "km,bom->bko", selector, part_left.reshape(own, order, order), preferred_element_type=jnp.float32
    ).astype(jnp.bfloat16)
    grad_left = sum_over_dp(part_left) * factor
    return (mixed, grad_tokens, grad_left, grad_right)


def solution(mesh):
    in_specs = (
        P("dp", "blk"),
        P("blk", None, None),
        P("blk", None, None),
        P("dp", "blk"),
        P("blk", "dp"),
        P(),
    )
    out_specs = (P("dp", "blk"), P("dp", "blk"), P("blk", None, None), P("blk", None, None))
    return jax.shard_map(local, mesh=mesh, in_specs=in_specs, out_specs=out_specs, check_vma=False)
```

```python
import math

import jax
import jax.numpy as jnp
import numpy as np
from jax import lax
from jax.experimental import pallas as pl
from jax.experimental.pallas import tpu as pltpu
from jax.sharding import PartitionSpec as P

keep_rate = 0.9
CHUNKS = 4
TILE = 512
VMEM_LIMIT = 60 * 1024 * 1024
FIRST_LAG = 3
SECOND_LAG = 2
ANY = pl.BlockSpec(memory_space=pl.ANY)
NT = (((1,), (1,)), ((), ()))
TN = (((0,), (0,)), ((), ()))
NN = (((1,), (0,)), ((), ()))


def dot(lhs, rhs, dims):
    return lax.dot_general(lhs, rhs, dims, preferred_element_type=jnp.float32)


class Plan:
    def __init__(self, rows, own, order, devices):
        self.rows, self.own, self.order, self.devices = rows, own, order, devices
        self.direct = (2 * own) % 16 == 0 and own >= 2
        self.pair = 2 if self.direct else own
        self.pairs = own // self.pair
        self.slots = devices if self.direct else 1
        quarter = max(devices // 4, 1)
        near, far = list(range(devices // 2)), list(range(devices // 2, devices))
        near = [hop for both in zip(near[:quarter], near[quarter:]) for hop in both]
        far = [hop for both in zip(far[:quarter], far[quarter:]) for hop in both]
        self.hops = [hop for both in zip(near, far) for hop in both]
        self.height = devices * own * own
        self.slot_height = self.height // self.slots
        self.width = own * order
        self.chunks = CHUNKS
        self.chunk = rows // self.chunks
        self.tile = math.gcd(self.chunk, TILE)
        self.steps = self.chunk // self.tile

    def token_spec(self, chunk):
        return pl.BlockSpec((self.tile, self.width), lambda i: (chunk * self.steps + i, 0))

    def slot_specs(self):
        return [pl.BlockSpec((self.slot_height, self.tile), lambda i: (0, i))] * self.slots

    def slot_shapes(self):
        return [jax.ShapeDtypeStruct((self.slot_height, self.chunk), jnp.bfloat16)] * self.slots

    def pair_rows(self, refs, pair):
        if self.pairs == 1 and self.slots == 1:
            return refs[0][...]
        size = self.pair * self.own
        return jnp.concatenate([ref[pair * size : (pair + 1) * size, :] for ref in refs], axis=0)


def whole(array):
    zeros = (0,) * array.ndim
    return pl.BlockSpec(array.shape, lambda i: zeros)


def call(body, plan, ins, in_specs, outs, out_specs, aliases, flops, scratch=()):
    size = sum(math.prod(o.shape) * o.dtype.itemsize for o in outs[: plan.slots]) * 4
    return pl.pallas_call(
        body,
        out_shape=outs,
        grid=(plan.steps,),
        in_specs=in_specs,
        out_specs=out_specs,
        scratch_shapes=scratch,
        input_output_aliases=aliases,
        compiler_params=pltpu.CompilerParams(vmem_limit_bytes=VMEM_LIMIT),
        cost_estimate=pl.CostEstimate(flops=flops, bytes_accessed=size, transcendentals=0),
    )(*ins)


def first_factor(plan, chunk, tokens, wide_left, after):
    def body(tokens_ref, left_ref, *refs):
        product = dot(left_ref[...], tokens_ref[...], NT).astype(jnp.bfloat16)
        for slot, ref in enumerate(refs[len(after) :]):
            ref[...] = product[slot * plan.slot_height : (slot + 1) * plan.slot_height, :]

    return call(
        body,
        plan,
        (tokens, wide_left, *after),
        [plan.token_spec(chunk), whole(wide_left), *[ANY] * len(after)],
        plan.slot_shapes(),
        plan.slot_specs(),
        {},
        2 * plan.height * plan.width * plan.chunk,
    )


def second_factor(plan, chunk, received, tokens, cotangent, keep_mask, spread, wide_right, state, after):
    slots, span = plan.slots, plan.pair * plan.order

    def body(*refs):
        got = refs[:slots]
        tokens_ref, cotangent_ref, mask_ref, spread_ref, right_ref = refs[slots : slots + 5]
        outs = refs[len(refs) - slots - 2 :]
        sent, mixed_ref, total_ref = outs[:slots], outs[slots], outs[slots + 1]

        @pl.when(pl.program_id(0) == 0)
        def _():
            if chunk == 0:
                total_ref[...] = jnp.zeros_like(total_ref)
            else:
                total_ref[...] = refs[slots + 6][...]

        mask = mask_ref[...].astype(jnp.float32).astype(jnp.bfloat16)
        for pair in range(plan.pairs):
            columns = slice(pair * span, (pair + 1) * span)
            kept = dot(mask, spread_ref[:, columns], TN) * jnp.float32(1.0 / keep_rate)
            rows = plan.pair_rows(got, pair)
            mixing = dot(rows, right_ref[pair], TN)
            cdf = 0.5 * (1.0 + lax.erf(mixing * jnp.float32(1.0 / math.sqrt(2.0))))
            pdf = jnp.exp(-0.5 * mixing * mixing) * jnp.float32(1.0 / math.sqrt(2.0 * math.pi))
            branch = kept * mixing * cdf
            mixed_ref[:, columns] = (tokens_ref[:, columns].astype(jnp.float32) + branch).astype(jnp.bfloat16)
            grad_mix = (cotangent_ref[:, columns].astype(jnp.float32) * kept * (cdf + mixing * pdf)).astype(
                jnp.bfloat16
            )
            total_ref[pair] += dot(rows, grad_mix, NN)
            back = dot(right_ref[pair], grad_mix, NT).astype(jnp.bfloat16)
            if plan.pairs == 1 and slots == 1:
                sent[0][...] = back
            else:
                size = plan.pair * plan.own
                for slot, ref in enumerate(sent):
                    ref[pair * size : (pair + 1) * size, :] = back[slot * size : (slot + 1) * size, :]

    ins = (*received, tokens, cotangent, keep_mask, spread, wide_right)
    in_specs = [
        *plan.slot_specs(),
        plan.token_spec(chunk),
        plan.token_spec(chunk),
        pl.BlockSpec((plan.own, plan.tile), lambda i: (0, chunk * plan.steps + i)),
        whole(spread),
        whole(wide_right),
    ]
    aliases = {}
    if state is not None:
        aliases = {len(ins): slots, len(ins) + 1: slots + 1}
        ins = (*ins, *state)
        in_specs += [ANY, whole(state[1])]
    ins = (*ins, *after)
    in_specs += [ANY] * len(after)
    outs = [
        *plan.slot_shapes(),
        jax.ShapeDtypeStruct(tokens.shape, jnp.bfloat16),
        jax.ShapeDtypeStruct((plan.pairs, plan.pair * plan.order, span), jnp.float32),
    ]
    out_specs = [*plan.slot_specs(), plan.token_spec(chunk), whole(outs[-1])]
    flops = 6 * plan.height * span * plan.chunk * 4
    result = call(body, plan, ins, in_specs, outs, out_specs, aliases, flops)
    return result[:slots], (result[slots], result[slots + 1])


def first_factor_back(plan, chunk, received, tokens, cotangent, wide_left, state):
    slots, own, order = plan.slots, plan.own, plan.order

    def body(*refs):
        got = refs[:slots]
        tokens_ref, cotangent_ref, left_ref = refs[slots : slots + 3]
        grad_ref, total_ref, scratch_ref = refs[-3:]
        step = pl.program_id(0)

        rows = got[0][...] if slots == 1 else jnp.concatenate([ref[...] for ref in got], axis=0)
        grad = dot(rows, left_ref[...], TN)
        grad_ref[...] = (cotangent_ref[...].astype(jnp.float32) + grad).astype(jnp.bfloat16)
        product = dot(rows, tokens_ref[...], NN)

        for block in range(own):
            part = product[:, block * order : (block + 1) * order]

            @pl.when(step == 0)
            def _():
                scratch_ref[block] = part

            @pl.when(step > 0)
            def _():
                scratch_ref[block] += part

        @pl.when(step == plan.steps - 1)
        def _():
            for block in range(own):
                part = scratch_ref[block, pl.ds(block, order, stride=own), :]
                total_ref[block] = part if chunk == 0 else part + refs[slots + 4][block]

    ins = (*received, tokens, cotangent, wide_left)
    in_specs = [*plan.slot_specs(), plan.token_spec(chunk), plan.token_spec(chunk), whole(wide_left)]
    aliases = {}
    if state is not None:
        aliases = {len(ins): 0, len(ins) + 1: 1}
        ins = (*ins, *state)
        in_specs += [ANY, whole(state[1])]
    outs = [
        jax.ShapeDtypeStruct(tokens.shape, jnp.bfloat16),
        jax.ShapeDtypeStruct((own, order, order), jnp.float32),
    ]
    out_specs = [plan.token_spec(chunk), whole(outs[1])]
    return call(
        body,
        plan,
        ins,
        in_specs,
        outs,
        out_specs,
        aliases,
        4 * plan.height * plan.width * plan.chunk,
        [pltpu.VMEM((own, plan.height, order), jnp.float32)],
    )


def exchange(plan, parts):
    if plan.direct:
        return [
            part if hop == 0 else lax.ppermute(part, "blk", [(i, i ^ hop) for i in range(plan.devices)])
            for hop, part in zip(plan.hops, parts)
        ]
    split = parts[0].reshape(plan.devices, plan.own * plan.own, plan.chunk)
    return [lax.all_to_all(split, "blk", 0, 0, tiled=True).reshape(plan.height, plan.chunk)]


def sum_over_dp(value):
    size = lax.axis_size("dp")
    if size == 2:
        return value.astype(jnp.float32) + lax.ppermute(value, "dp", [(0, 1), (1, 0)]).astype(jnp.float32)
    return lax.psum(value, "dp").astype(jnp.float32)


def local(tokens, left, right, cotangent, keep_mask, channel_order):
    rows, (own, order, _) = tokens.shape[0], left.shape
    devices = lax.axis_size("blk")
    plan = Plan(rows, own, order, devices)
    pair, pairs, span = plan.pair, plan.pairs, plan.pair * order
    partner = place = lax.iota(jnp.int32, devices)
    if plan.direct:
        place = jnp.take(jnp.array(np.argsort(plan.hops), jnp.int32), place ^ lax.axis_index("blk"))
        partner = jnp.array(plan.hops, jnp.int32) ^ lax.axis_index("blk")
    factor = 1.0 / math.sqrt(rows * lax.axis_size("dp"))

    selector = (channel_order[:, None] == lax.broadcasted_iota(jnp.int32, (order, order), 1)).astype(jnp.bfloat16)
    unpermuted_left = jnp.einsum("km,bko->obm", selector, left, preferred_element_type=jnp.float32).astype(jnp.bfloat16)
    slotted_left = jnp.take(unpermuted_left.reshape(devices, own, own, order), partner, axis=0)
    eye = jnp.eye(own, dtype=jnp.bfloat16)
    wide_left = (slotted_left.reshape(order, 1, own, order) * eye[None, :, :, None]).reshape(plan.height, plan.width)

    slotted_right = jnp.take(right.reshape(own, devices, own, order), partner, axis=1)
    slotted_right = slotted_right.reshape(pairs, pair, devices, own, order).transpose(0, 2, 1, 3, 4)
    eye_pair = jnp.eye(pair, dtype=jnp.bfloat16)
    wide_right = (slotted_right[:, :, :, :, None, :] * eye_pair[None, None, :, None, :, None]).reshape(
        pairs, pair * order, span
    )
    spread = jnp.repeat(eye, order, axis=1)

    forward, backward, state = [], [], None
    for step in range(plan.chunks + SECOND_LAG):
        if step < plan.chunks:
            after = backward[step - FIRST_LAG][1:] if step >= FIRST_LAG else []
            forward.append(exchange(plan, first_factor(plan, step, tokens, wide_left, after)))
        chunk = step - SECOND_LAG
        if chunk >= 0:
            after = backward[chunk - SECOND_LAG][1:] if chunk >= SECOND_LAG else []
            sent, state = second_factor(
                plan, chunk, forward[chunk], tokens, cotangent, keep_mask, spread, wide_right, state, after
            )
            backward.append(exchange(plan, sent))
    mixed, wide_total = state

    split_total = wide_total.reshape(pairs, devices, pair, own, pair, order)
    part_right = jnp.stack([split_total[:, :, jj, :, jj, :] for jj in range(pair)], axis=1)
    part_right = jnp.take(part_right.reshape(own, devices, own, order), place, axis=1).reshape(own, order, order)
    grad_right = sum_over_dp(part_right.astype(jnp.bfloat16)) * factor

    state = None
    for chunk in range(plan.chunks):
        state = first_factor_back(plan, chunk, backward[chunk], tokens, cotangent, wide_left, state)
    grad_tokens, part_left = state
    part_left = jnp.take(part_left.astype(jnp.bfloat16).reshape(own, devices, own, order), place, axis=1)
    part_left = jnp.einsum(
        "km,bom->bko", selector, part_left.reshape(own, order, order), preferred_element_type=jnp.float32
    ).astype(jnp.bfloat16)
    grad_left = sum_over_dp(part_left) * factor
    return (mixed, grad_tokens, grad_left, grad_right)


def solution(mesh):
    in_specs = (
        P("dp", "blk"),
        P("blk", None, None),
        P("blk", None, None),
        P("dp", "blk"),
        P("blk", "dp"),
        P(),
    )
    out_specs = (P("dp", "blk"), P("dp", "blk"), P("blk", None, None), P("blk", None, None))
    return jax.shard_map(local, mesh=mesh, in_specs=in_specs, out_specs=out_specs, check_vma=False)
```

```python
import copy
import math

import jax
import jax.numpy as jnp
import numpy as np
from jax import lax
from jax.experimental import pallas as pl
from jax.experimental.pallas import tpu as pltpu
from jax.sharding import PartitionSpec as P

keep_rate = 0.9
SHARES = (3,8,8,5)
TILE = 512
VMEM_LIMIT = 60 * 1024 * 1024
SECOND_LAG = 2
ANY = pl.BlockSpec(memory_space=pl.ANY)
NT = (((1,), (1,)), ((), ()))
TN = (((0,), (0,)), ((), ()))
NN = (((1,), (0,)), ((), ()))


def dot(lhs, rhs, dims):
    return lax.dot_general(lhs, rhs, dims, preferred_element_type=jnp.float32)


class Plan:
    def __init__(self, rows, own, order, devices):
        self.rows, self.own, self.order, self.devices = rows, own, order, devices
        self.direct = (2 * own) % 16 == 0 and own >= 2
        self.pair = 2 if self.direct else own
        self.pairs = own // self.pair
        self.slots = devices if self.direct else 1
        quarter = max(devices // 4, 1)
        near, far = list(range(devices // 2)), list(range(devices // 2, devices))
        near = [hop for both in zip(near[:quarter], near[quarter:]) for hop in both]
        far = [hop for both in zip(far[:quarter], far[quarter:]) for hop in both]
        self.hops = [hop for both in zip(near, far) for hop in both]
        self.height = devices * own * own
        self.slot_height = self.height // self.slots
        self.width = own * order
        self.chunks = len(SHARES)
        self.tile = math.gcd(rows // sum(SHARES), TILE)

    def part(self, chunk):
        plan, unit = copy.copy(self), self.rows // sum(SHARES)
        plan.chunk = SHARES[chunk] * unit
        plan.steps = plan.chunk // plan.tile
        plan.first = sum(SHARES[:chunk]) * unit // plan.tile
        return plan

    def token_spec(self):
        return pl.BlockSpec((self.tile, self.width), lambda i: (self.first + i, 0))

    def slot_specs(self):
        return [pl.BlockSpec((self.slot_height, self.tile), lambda i: (0, i))] * self.slots

    def slot_shapes(self):
        return [jax.ShapeDtypeStruct((self.slot_height, self.chunk), jnp.bfloat16)] * self.slots

    def pair_rows(self, refs, pair):
        if self.pairs == 1 and self.slots == 1:
            return refs[0][...]
        size = self.pair * self.own
        return jnp.concatenate([ref[pair * size : (pair + 1) * size, :] for ref in refs], axis=0)


def whole(array):
    zeros = (0,) * array.ndim
    return pl.BlockSpec(array.shape, lambda i: zeros)


def call(body, plan, ins, in_specs, outs, out_specs, aliases, flops, scratch=()):
    size = sum(math.prod(o.shape) * o.dtype.itemsize for o in outs[: plan.slots]) * 4
    return pl.pallas_call(
        body,
        out_shape=outs,
        grid=(plan.steps,),
        in_specs=in_specs,
        out_specs=out_specs,
        scratch_shapes=scratch,
        input_output_aliases=aliases,
        compiler_params=pltpu.CompilerParams(vmem_limit_bytes=VMEM_LIMIT),
        cost_estimate=pl.CostEstimate(flops=flops, bytes_accessed=size, transcendentals=0),
    )(*ins)


def first_factor(plan, tokens, wide_left):
    def body(tokens_ref, left_ref, *refs):
        product = dot(left_ref[...], tokens_ref[...], NT).astype(jnp.bfloat16)
        for slot, ref in enumerate(refs):
            ref[...] = product[slot * plan.slot_height : (slot + 1) * plan.slot_height, :]

    return call(
        body,
        plan,
        (tokens, wide_left),
        [plan.token_spec(), whole(wide_left)],
        plan.slot_shapes(),
        plan.slot_specs(),
        {},
        2 * plan.height * plan.width * plan.chunk,
    )


def second_factor(plan, chunk, received, tokens, cotangent, keep_mask, spread, wide_right, state, after):
    slots, span = plan.slots, plan.pair * plan.order

    def body(*refs):
        got = refs[:slots]
        tokens_ref, cotangent_ref, mask_ref, spread_ref, right_ref = refs[slots : slots + 5]
        outs = refs[len(refs) - slots - 2 :]
        sent, mixed_ref, total_ref = outs[:slots], outs[slots], outs[slots + 1]

        @pl.when(pl.program_id(0) == 0)
        def _():
            if chunk == 0:
                total_ref[...] = jnp.zeros_like(total_ref)
            else:
                total_ref[...] = refs[slots + 6][...]

        mask = mask_ref[...].astype(jnp.float32).astype(jnp.bfloat16)
        for pair in range(plan.pairs):
            columns = slice(pair * span, (pair + 1) * span)
            kept = dot(mask, spread_ref[:, columns], TN) * jnp.float32(1.0 / keep_rate)
            rows = plan.pair_rows(got, pair)
            mixing = dot(rows, right_ref[pair], TN)
            cdf = 0.5 * (1.0 + lax.erf(mixing * jnp.float32(1.0 / math.sqrt(2.0))))
            pdf = jnp.exp(-0.5 * mixing * mixing) * jnp.float32(1.0 / math.sqrt(2.0 * math.pi))
            branch = kept * mixing * cdf
            mixed_ref[:, columns] = (tokens_ref[:, columns].astype(jnp.float32) + branch).astype(jnp.bfloat16)
            grad_mix = (cotangent_ref[:, columns].astype(jnp.float32) * kept * (cdf + mixing * pdf)).astype(
                jnp.bfloat16
            )
            total_ref[pair] += dot(rows, grad_mix, NN)
            back = dot(right_ref[pair], grad_mix, NT).astype(jnp.bfloat16)
            if plan.pairs == 1 and slots == 1:
                sent[0][...] = back
            else:
                size = plan.pair * plan.own
                for slot, ref in enumerate(sent):
                    ref[pair * size : (pair + 1) * size, :] = back[slot * size : (slot + 1) * size, :]

    ins = (*received, tokens, cotangent, keep_mask, spread, wide_right)
    in_specs = [
        *plan.slot_specs(),
        plan.token_spec(),
        plan.token_spec(),
        pl.BlockSpec((plan.own, plan.tile), lambda i: (0, plan.first + i)),
        whole(spread),
        whole(wide_right),
    ]
    aliases = {}
    if state is not None:
        aliases = {len(ins): slots, len(ins) + 1: slots + 1}
        ins = (*ins, *state)
        in_specs += [ANY, whole(state[1])]
    ins = (*ins, *after)
    in_specs += [ANY] * len(after)
    outs = [
        *plan.slot_shapes(),
        jax.ShapeDtypeStruct(tokens.shape, jnp.bfloat16),
        jax.ShapeDtypeStruct((plan.pairs, plan.pair * plan.order, span), jnp.float32),
    ]
    out_specs = [*plan.slot_specs(), plan.token_spec(), whole(outs[-1])]
    flops = 6 * plan.height * span * plan.chunk * 4
    result = call(body, plan, ins, in_specs, outs, out_specs, aliases, flops)
    return result[:slots], (result[slots], result[slots + 1])


def first_factor_back(plan, chunk, received, tokens, cotangent, wide_left, state):
    slots, own, order = plan.slots, plan.own, plan.order

    def body(*refs):
        got = refs[:slots]
        tokens_ref, cotangent_ref, left_ref = refs[slots : slots + 3]
        grad_ref, total_ref, scratch_ref = refs[-3:]
        step = pl.program_id(0)

        rows = got[0][...] if slots == 1 else jnp.concatenate([ref[...] for ref in got], axis=0)
        grad = dot(rows, left_ref[...], TN)
        grad_ref[...] = (cotangent_ref[...].astype(jnp.float32) + grad).astype(jnp.bfloat16)
        product = dot(rows, tokens_ref[...], NN)

        for block in range(own):
            part = product[:, block * order : (block + 1) * order]

            @pl.when(step == 0)
            def _():
                scratch_ref[block] = part

            @pl.when(step > 0)
            def _():
                scratch_ref[block] += part

        @pl.when(step == plan.steps - 1)
        def _():
            for block in range(own):
                part = scratch_ref[block, pl.ds(block, order, stride=own), :]
                total_ref[block] = part if chunk == 0 else part + refs[slots + 4][block]

    ins = (*received, tokens, cotangent, wide_left)
    in_specs = [*plan.slot_specs(), plan.token_spec(), plan.token_spec(), whole(wide_left)]
    aliases = {}
    if state is not None:
        aliases = {len(ins): 0, len(ins) + 1: 1}
        ins = (*ins, *state)
        in_specs += [ANY, whole(state[1])]
    outs = [
        jax.ShapeDtypeStruct(tokens.shape, jnp.bfloat16),
        jax.ShapeDtypeStruct((own, order, order), jnp.float32),
    ]
    out_specs = [plan.token_spec(), whole(outs[1])]
    return call(
        body,
        plan,
        ins,
        in_specs,
        outs,
        out_specs,
        aliases,
        4 * plan.height * plan.width * plan.chunk,
        [pltpu.VMEM((own, plan.height, order), jnp.float32)],
    )


def exchange(plan, parts):
    if plan.direct:
        return [
            part if hop == 0 else lax.ppermute(part, "blk", [(i, i ^ hop) for i in range(plan.devices)])
            for hop, part in zip(plan.hops, parts)
        ]
    split = parts[0].reshape(plan.devices, plan.own * plan.own, plan.chunk)
    return [lax.all_to_all(split, "blk", 0, 0, tiled=True).reshape(plan.height, plan.chunk)]


def sum_over_dp(value):
    size = lax.axis_size("dp")
    if size == 2:
        return value.astype(jnp.float32) + lax.ppermute(value, "dp", [(0, 1), (1, 0)]).astype(jnp.float32)
    return lax.psum(value, "dp").astype(jnp.float32)


def local(tokens, left, right, cotangent, keep_mask, channel_order):
    rows, (own, order, _) = tokens.shape[0], left.shape
    devices = lax.axis_size("blk")
    plan = Plan(rows, own, order, devices)
    pair, pairs, span = plan.pair, plan.pairs, plan.pair * order
    partner = place = lax.iota(jnp.int32, devices)
    if plan.direct:
        place = jnp.take(jnp.array(np.argsort(plan.hops), jnp.int32), place ^ lax.axis_index("blk"))
        partner = jnp.array(plan.hops, jnp.int32) ^ lax.axis_index("blk")
    factor = 1.0 / math.sqrt(rows * lax.axis_size("dp"))

    selector = (channel_order[:, None] == lax.broadcasted_iota(jnp.int32, (order, order), 1)).astype(jnp.bfloat16)
    unpermuted_left = jnp.einsum("km,bko->obm", selector, left, preferred_element_type=jnp.float32).astype(jnp.bfloat16)
    slotted_left = jnp.take(unpermuted_left.reshape(devices, own, own, order), partner, axis=0)
    eye = jnp.eye(own, dtype=jnp.bfloat16)
    wide_left = (slotted_left.reshape(order, 1, own, order) * eye[None, :, :, None]).reshape(plan.height, plan.width)

    slotted_right = jnp.take(right.reshape(own, devices, own, order), partner, axis=1)
    slotted_right = slotted_right.reshape(pairs, pair, devices, own, order).transpose(0, 2, 1, 3, 4)
    eye_pair = jnp.eye(pair, dtype=jnp.bfloat16)
    wide_right = (slotted_right[:, :, :, :, None, :] * eye_pair[None, None, :, None, :, None]).reshape(
        pairs, pair * order, span
    )
    spread = jnp.repeat(eye, order, axis=1)

    forward, backward, state = [], [], None
    for step in range(plan.chunks + SECOND_LAG):
        if step < plan.chunks:
            part = plan.part(step)
            forward.append(exchange(part, first_factor(part, tokens, wide_left)))
        chunk = step - SECOND_LAG
        if chunk >= 0:
            after = backward[chunk - SECOND_LAG][1:] if chunk >= SECOND_LAG else []
            part = plan.part(chunk)
            sent, state = second_factor(
                part, chunk, forward[chunk], tokens, cotangent, keep_mask, spread, wide_right, state, after
            )
            backward.append(exchange(part, sent))
    mixed, wide_total = state

    split_total = wide_total.reshape(pairs, devices, pair, own, pair, order)
    part_right = jnp.stack([split_total[:, :, jj, :, jj, :] for jj in range(pair)], axis=1)
    part_right = jnp.take(part_right.reshape(own, devices, own, order), place, axis=1).reshape(own, order, order)
    grad_right = sum_over_dp(part_right.astype(jnp.bfloat16)) * factor

    state = None
    for chunk in range(plan.chunks):
        state = first_factor_back(plan.part(chunk), chunk, backward[chunk], tokens, cotangent, wide_left, state)
    grad_tokens, part_left = state
    part_left = jnp.take(part_left.astype(jnp.bfloat16).reshape(own, devices, own, order), place, axis=1)
    part_left = jnp.einsum(
        "km,bom->bko", selector, part_left.reshape(own, order, order), preferred_element_type=jnp.float32
    ).astype(jnp.bfloat16)
    grad_left = sum_over_dp(part_left) * factor
    return (mixed, grad_tokens, grad_left, grad_right)


def solution(mesh):
    in_specs = (
        P("dp", "blk"),
        P("blk", None, None),
        P("blk", None, None),
        P("dp", "blk"),
        P("blk", "dp"),
        P(),
    )
    out_specs = (P("dp", "blk"), P("dp", "blk"), P("blk", None, None), P("blk", None, None))
    return jax.shard_map(local, mesh=mesh, in_specs=in_specs, out_specs=out_specs, check_vma=False)
```
